32 devices in a mesh: seq: 4 (over x, core), head: 8 (over z, y).
Axes of the slice: x: 2, y: 2, z: 4, core: 2. Of those that a mesh axis runs over, the one named last changes fastest.
Arguments:
- queries: bfloat16 [4096, 2560], P('seq', 'head'), may hold values from -6 to 6
- key_vectors: bfloat16 [4096, 2560], P('seq', 'head'), may hold values from -6 to 6
- value_vectors: bfloat16 [4096, 2560], P('seq', 'head'), may hold values from -6 to 6
- fast_gate: float32 [8, 320, 320], P('head'), may hold values from -0.3125 to 0.3125
- fast_up: float32 [8, 320, 320], P('head'), may hold values from -0.3125 to 0.3125
- fast_down: float32 [8, 320, 320], P('head'), may hold values from -1 to 1
- step_sizes: float32 [8], P('head'), may hold values from 0.2 to 1
- out_gain: float32 [2560], P('head'), may hold values from 0.25 to 1.75
Outputs:
- layer_output: float32 [4, 1024, 2560], P(None, 'seq', 'head')
The draws below stay inside these ranges and needn't reach their ends.
All inputs are finite; a program needn't handle non-finite values.
Results may differ from the reference program's by a relative error of at most 0.038.
Values may be sent and summed in bfloat16 or wider, within the bound.
A program may use at most 64 MiB of HBM per device.

```python
import math
import jax
import jax.numpy as jnp
from jax import lax

DH = 320
TOK_DEV = 1024
GROUPS = 2
NS_ITERS = 4
HEADS = 8
D = 2560
TOKENS = 4096
WINDOW = 512
N_SEQ = 4


def drawn_pair(key):
    base = jax.random.fold_in(key, 11)
    first_key, second_key = jax.random.split(base, 2)
    query_rows = jnp.clip(jax.random.normal(first_key, (TOKENS, D)), -6.0, 6.0)
    key_rows = jnp.clip(jax.random.normal(second_key, (TOKENS, D)), -6.0, 6.0)
    return (query_rows, key_rows)


def draw_queries(key, part):
    return drawn_pair(key)[0].astype(jnp.bfloat16)


def draw_key_vectors(key, part):
    return drawn_pair(key)[1].astype(jnp.bfloat16)


def draw_fast_down(key, part):
    inner = jax.random.fold_in(key, 23)
    factor = 1.0 + 2.0 * jnp.arange(HEADS) / max(HEADS - 1, 1)
    entries = jax.random.normal(inner, (HEADS, DH, DH))
    entries = entries * factor[:, None, None] / jnp.sqrt(DH * 1.0)
    return jnp.clip(entries, -1.0, 1.0).astype(jnp.float32)


def block_scale(rng, extent, shards, least, top_value):
    gain, own = 1.0, jax.random.fold_in(rng, 6)
    for dim, blocks in shards:
        steps = jnp.exp(jax.random.uniform(jax.random.fold_in(own, dim), (blocks,), jnp.float32, least / len(shards), top_value / len(shards)))
        gain = gain * jnp.repeat(steps, extent[dim] // blocks).reshape([-1 if axis == dim else 1 for axis in range(len(extent))])
    return gain


def normal_values(stream_key, shape, scale, bound, pieces=(), kind=jnp.bfloat16):
    array = jax.random.normal(stream_key, shape, jnp.float32) * scale
    if len(pieces) > 0:
        array = block_scale(stream_key, shape, pieces, -0.22, 0.18) * array
    return jnp.clip(array, min=-bound, max=bound).astype(kind)


def setup_inputs(seed: int = 0) -> dict:
    streams_of = jax.random.split(jax.random.key(seed), 9)
    return {
        "queries": draw_queries(jax.random.fold_in(streams_of[8], 71), 0),
        "key_vectors": draw_key_vectors(jax.random.fold_in(streams_of[8], 71), 0),
        "value_vectors": normal_values(streams_of[2], (TOKENS, D), 1.0, 6.0, ((0, 4), (1, 8))),
        "fast_gate": normal_values(streams_of[3], (HEADS, DH, DH), DH ** -0.5, 0.3125, ((0, 8),), jnp.float32),
        "fast_up": normal_values(streams_of[4], (HEADS, DH, DH), DH ** -0.5, 0.3125, ((0, 8),), jnp.float32),
        "fast_down": draw_fast_down(jax.random.fold_in(streams_of[8], 71), 0),
        "step_sizes": jnp.clip(jnp.exp(math.log(1.0) - 1.609438 * jax.random.uniform(streams_of[6], (HEADS,), jnp.float32) ** block_scale(streams_of[6], (HEADS,), ((0, 8),), -0.2, 0.2)), 0.2, 1.0),
        "out_gain": jnp.clip(1.0 + 0.15 * jax.random.normal(streams_of[7], (D,), jnp.float32), 0.25, 1.75),
    }


newton_coefs = (3.4445, -4.775, 2.0315)

def attention_rows(queries, key_vectors, value_vectors):
    width = queries.shape[1]
    block = min(512, TOKENS)
    scale = 1.0 / math.sqrt(DH)
    padded_keys = jnp.concatenate([jnp.zeros((WINDOW, width), jnp.bfloat16), key_vectors], 0)
    padded_values = jnp.concatenate([jnp.zeros((WINDOW, width), jnp.bfloat16), value_vectors], 0)

    def one_block(start):
        query_block = lax.dynamic_slice_in_dim(queries, start, block, 0).astype(jnp.float32).reshape(block, HEADS, DH)
        key_block = lax.dynamic_slice_in_dim(padded_keys, start, WINDOW + block, 0).astype(jnp.float32).reshape(WINDOW + block, HEADS, DH)
        value_block = lax.dynamic_slice_in_dim(padded_values, start, WINDOW + block, 0).astype(jnp.float32).reshape(WINDOW + block, HEADS, DH)
        scores = jnp.einsum('qhd,khd->hqk', query_block, key_block) * scale
        query_pos = start + jnp.arange(block, dtype=jnp.int32)
        key_pos = start - WINDOW + jnp.arange(WINDOW + block, dtype=jnp.int32)
        allowed = (key_pos[None, :] <= query_pos[:, None]) & (key_pos[None, :] > query_pos[:, None] - WINDOW) & (key_pos[None, :] >= 0)
        scores = jnp.where(allowed[None], scores, -1e+30)
        highest = lax.optimization_barrier(jnp.max(scores, -1, keepdims=True))
        expo = jnp.where(allowed[None], jnp.exp(scores - highest), 0.0)
        probs = (expo / lax.optimization_barrier(jnp.sum(expo, -1, keepdims=True))).astype(jnp.bfloat16)
        mixed = jnp.einsum('hqk,khd->qhd', probs.astype(jnp.float32), value_block)
        return mixed.reshape(block, width).astype(jnp.bfloat16)
    starts = jnp.arange(TOKENS // block, dtype=jnp.int32) * block
    return lax.map(one_block, starts).reshape(TOKENS, width)

def rms_rows(rows):
    rows = rows.astype(jnp.float32)
    return (rows * lax.rsqrt(lax.optimization_barrier(jnp.mean(rows * rows, -1, keepdims=True)) + 1e-06)).astype(jnp.bfloat16)

def matmul(left, right):
    return jnp.dot(left, right, preferred_element_type=jnp.float32)

def group_gradients(weights, normed_keys, targets):
    rounded = weights.astype(jnp.bfloat16)
    gate = matmul(normed_keys, rounded[0])
    upward = matmul(normed_keys, rounded[1])
    active = jax.nn.silu(gate)
    hidden = (active * upward).astype(jnp.bfloat16)
    negative = -targets
    back_hidden = matmul(negative, rounded[2].T)
    sigma = jax.nn.sigmoid(gate)
    slope = sigma * (1.0 + gate * (1.0 - sigma))
    grad_gate = (back_hidden * upward * slope).astype(jnp.bfloat16)
    grad_upward = (back_hidden * active).astype(jnp.bfloat16)
    return jnp.stack([matmul(normed_keys.T, grad_gate), matmul(normed_keys.T, grad_upward), matmul(hidden.T, negative)])

def orthogonalize(grads):
    first, second, third = newton_coefs
    highest = lax.Precision.HIGHEST
    total = lax.optimization_barrier(jnp.sum(grads * grads, axis=(1, 2), keepdims=True))
    current = grads * lax.rsqrt(total + 1e-06)
    for repeat in range(NS_ITERS):
        gram = jnp.einsum('mij,mkj->mik', current, current, precision=highest)
        square = jnp.einsum('mij,mjk->mik', gram, gram, precision=highest)
        mixing = second * gram + third * square
        current = first * current + jnp.einsum('mij,mjk->mik', mixing, current, precision=highest)
    return current

def apply_fast(weights, normed_queries):
    rounded = weights.astype(jnp.bfloat16)
    hidden = (jax.nn.silu(matmul(normed_queries, rounded[0])) * matmul(normed_queries, rounded[1])).astype(jnp.bfloat16)
    return matmul(hidden, rounded[2])

def one_head(items):
    normed_q, normed_k, targets, weights, rate = items
    span = TOKENS // GROUPS
    results = []
    for group_index in range(GROUPS):
        start = group_index * span
        grads = group_gradients(weights, normed_k[start:start + span], targets[start:start + span])
        weights = weights - rate * orthogonalize(grads)
        results.append(apply_fast(weights, normed_q[start:start + span]))
    return jnp.concatenate(results, 0)

def per_head(tensor):
    return tensor.reshape(TOKENS, HEADS, DH).transpose(1, 0, 2)

def reference(queries, key_vectors, value_vectors, fast_gate, fast_up, fast_down, step_sizes, out_gain):
    attended = attention_rows(queries, key_vectors, value_vectors)
    normed_q = rms_rows(per_head(queries))
    normed_k = rms_rows(per_head(key_vectors))
    targets = per_head(value_vectors)
    weights = jnp.stack([fast_gate, fast_up, fast_down], 1)
    fast_out = lax.map(one_head, (normed_q, normed_k, targets, weights, step_sizes))
    fast_out = fast_out.transpose(1, 0, 2).reshape(TOKENS, D)
    totals = lax.optimization_barrier(jnp.sum(fast_out * fast_out, -1, keepdims=True))
    mixed = attended.astype(jnp.float32) + out_gain * fast_out * lax.rsqrt(totals / D + 1e-06)
    return mixed.reshape(N_SEQ, TOK_DEV, D)
```

```python
import functools
import math

import jax
import jax.numpy as jnp
from jax import lax
from jax.experimental import pallas as pl
from jax.experimental.pallas import tpu as pltpu
from jax.sharding import PartitionSpec as P

GROUPS = 2
NS_ITERS = 4
LANES = 128

newton_coefs = (3.4445, -4.775, 2.0315)
MESH = pl.DeviceIdType.MESH
BF = jnp.bfloat16
F32 = jnp.float32


def dot(left, right, left_dim, right_dim):
    return lax.dot_general(
        left, right, (((left_dim,), (right_dim,)), ((), ())), preferred_element_type=F32
    )


def rms_rows(rows):
    rows = rows.astype(F32)
    return (rows * lax.rsqrt(jnp.mean(rows * rows, -1, keepdims=True) + 1e-06)).astype(BF)


def kernel(
    seq_count,
    head_count,
    q_ref,
    k_ref,
    v_ref,
    gate_ref,
    up_ref,
    down_ref,
    step_ref,
    gain_ref,
    out_ref,
    q_all,
    att_own,
    att_all,
    tail_k,
    tail_v,
    key_t,
    val_t,
    grad_f,
    grad_b,
    grad_in,
    sums,
    weights,
    fast,
    squares,
    send_q,
    recv_q,
    send_att,
    recv_att,
    send_tail,
    recv_tail,
    send_part,
    recv_part,
    send_sum,
    recv_sum,
    send_cross,
    send_sq,
    recv_sq,
):
    rows, dh = q_ref.shape
    window = rows // 2
    members = seq_count // GROUPS
    out_rows = rows // seq_count
    group_rows = rows // GROUPS
    chunk = grad_in.shape[1]
    width = dh * head_count
    me = lax.axis_index("seq")
    head = lax.axis_index("head")
    own_group = me // members
    own_member = lax.rem(me, members)

    def remote(src, dst, send, recv, seq, hd):
        return pltpu.make_async_remote_copy(
            src_ref=src,
            dst_ref=dst,
            send_sem=send,
            recv_sem=recv,
            device_id=(seq, hd),
            device_id_type=MESH,
        )

    def rows_of(index, size):
        return pl.ds(pl.multiple_of(index * size, size), size)

    barrier = pltpu.get_barrier_semaphore()
    for d in range(1, seq_count):
        pl.semaphore_signal(
            barrier, inc=1, device_id=(lax.rem(me + d, seq_count), head), device_id_type=MESH
        )
    for d in range(1, head_count):
        pl.semaphore_signal(
            barrier, inc=1, device_id=(me, lax.rem(head + d, head_count)), device_id_type=MESH
        )

    key_t[...] = jnp.transpose(rms_rows(k_ref[...]).astype(F32)).astype(BF)
    val_t[...] = jnp.transpose(-v_ref[...].astype(F32)).astype(BF)
    weights[0] = gate_ref[0]
    weights[1] = up_ref[0]
    weights[2] = down_ref[0]
    q_all[me] = q_ref[rows_of(me, out_rows), :]
    spare = members * chunk - 3 * dh
    if spare:
        grad_f[3 * dh :, :] = jnp.zeros((spare, dh), F32)
        grad_b[3 * dh :, :] = jnp.zeros((spare, dh), BF)

    @pl.when(me == 0)
    def _():
        tail_k[...] = jnp.zeros(tail_k.shape, BF)
        tail_v[...] = jnp.zeros(tail_v.shape, BF)

    pl.semaphore_wait(barrier, seq_count + head_count - 2)

    def q_copy(d, slot):
        return remote(
            q_ref.at[pl.ds(d * out_rows, out_rows), :],
            q_all.at[slot],
            send_q.at[d],
            recv_q.at[slot],
            d,
            head,
        )

    def tail_copy(which, target):
        source = (k_ref, v_ref)[which]
        landing = (tail_k, tail_v)[which]
        return remote(
            source.at[pl.ds(rows - window, window), :],
            landing,
            send_tail.at[which],
            recv_tail.at[which],
            target,
            head,
        )

    def send_inputs():
        @pl.when(me < seq_count - 1)
        def _():
            tail_copy(0, me + 1).start()
            tail_copy(1, me + 1).start()

        for d in range(seq_count):

            @pl.when(me != d)
            def _():
                q_copy(d, me).start()

    scale = 1.0 / math.sqrt(dh)
    block = min(256, window)

    def attend(start):
        queries = q_ref[start : start + block, :]
        if start < window:
            keys = jnp.concatenate([tail_k[start:, :], k_ref[: start + block, :]], 0)
            values = jnp.concatenate([tail_v[start:, :], v_ref[: start + block, :]], 0)
        else:
            keys = k_ref[start - window : start + block, :]
            values = v_ref[start - window : start + block, :]
        scores = dot(queries, keys, 1, 1) * scale
        row = lax.broadcasted_iota(jnp.int32, scores.shape, 0)
        col = lax.broadcasted_iota(jnp.int32, scores.shape, 1)
        allowed = (col <= row + window) & (col > row)
        if start < window:
            allowed = allowed & (col >= jnp.where(me == 0, window - start, 0))
        scores = jnp.where(allowed, scores, -1e30)
        highest = jnp.max(scores, -1, keepdims=True)
        expo = jnp.where(allowed, jnp.exp(scores - highest), 0.0)
        probs = (expo / jnp.sum(expo, -1, keepdims=True)).astype(BF)
        att_own[start : start + block, :] = dot(probs, values, 1, 0).astype(BF)

    def att_copy(d, slot):
        return remote(
            att_own.at[pl.ds(d * out_rows, out_rows), :],
            att_all.at[slot],
            send_att.at[d],
            recv_att.at[slot],
            d,
            head,
        )

    def attend_half(first):
        begin = 0 if first else window
        if first:

            @pl.when(me > 0)
            def _():
                tail_copy(0, me).wait_recv()
                tail_copy(1, me).wait_recv()

        for start in range(begin, begin + window, block):
            attend(start)
        for d in range(begin // out_rows, (begin + window) // out_rows):

            @pl.when(me != d)
            def _():
                att_copy(d, me).start()

            @pl.when(me == d)
            def _():
                att_all[d] = att_own[d * out_rows : (d + 1) * out_rows, :]

    token_block = min(256, rows)

    def gradients():
        wb = [weights[i].astype(BF) for i in range(3)]
        totals = [None] * 3
        for start in range(0, rows, token_block):
            keys = key_t[:, start : start + token_block]
            values = val_t[:, start : start + token_block]
            gate = dot(wb[0], keys, 0, 0)
            upward = dot(wb[1], keys, 0, 0)
            back = dot(wb[2], values, 1, 0)
            sigma = jax.nn.sigmoid(gate)
            active = gate * sigma
            hidden = (active * upward).astype(BF)
            slope = sigma * (1.0 + gate * (1.0 - sigma))
            grad_gate = (back * upward * slope).astype(BF)
            grad_up = (back * active).astype(BF)
            parts = [
                dot(keys, grad_gate, 1, 1),
                dot(keys, grad_up, 1, 1),
                dot(hidden, values, 1, 1),
            ]
            totals = [p if t is None else t + p for t, p in zip(totals, parts)]
        for i in range(3):
            grad_f[i * dh : (i + 1) * dh, :] = totals[i]
            grad_b[i * dh : (i + 1) * dh, :] = totals[i].astype(BF)

    def part_copy(group, target, slot):
        return remote(
            grad_b.at[pl.ds(target * chunk, chunk), :],
            grad_in.at[slot],
            send_part.at[target],
            recv_part.at[slot],
            group * members + target,
            head,
        )

    def sum_copy(group, piece, send, seq):
        place = sums.at[group, rows_of(piece, chunk), :]
        return remote(place, place, send, recv_sum.at[group, piece], seq, head)

    def spread(group):
        for m in range(members):

            @pl.when(own_member != m)
            def _():
                sum_copy(
                    group, own_member, send_sum.at[group, m], own_group * members + m
                ).start()

    def group_sums(group):
        gradients()
        for m in range(members):

            @pl.when(own_member != m)
            def _():
                part_copy(group, m, own_member).start()

        place = rows_of(own_member, chunk)
        grad_in[own_member] = jnp.zeros(grad_in.shape[1:], BF)
        for m in range(members):

            @pl.when(own_member != m)
            def _():
                part_copy(group, m, m).wait_recv()

        total = grad_f[place, :]
        for m in range(members):
            total = total + grad_in[m].astype(F32)
        sums[group, place, :] = total.astype(BF)
        for other in range(GROUPS):
            if other != group:
                sum_copy(
                    group, own_member, send_cross.at[other], other * members + own_member
                ).start()
        spread(group)

    def collect_sums(group):
        @pl.when(own_group != group)
        def _():
            sum_copy(group, own_member, send_cross.at[group], me).wait_recv()
            spread(group)

        for m in range(members):

            @pl.when(own_member != m)
            def _():
                sum_copy(group, m, send_cross.at[group], me).wait_recv()

    def update(group):
        first, second, third = newton_coefs
        current = []
        for i in range(3):
            grads = sums[group, i * dh : (i + 1) * dh, :].astype(F32)
            total = jnp.sum(jnp.sum(grads * grads, 1, keepdims=True), 0, keepdims=True)
            current.append(grads * lax.rsqrt(total + 1e-06))
        for repeat in range(NS_ITERS):
            low = [x.astype(BF) for x in current]
            gram = [dot(x, x, 1, 1) for x in low]
            gram_low = [a.astype(BF) for a in gram]
            square = [dot(a, a, 1, 0) for a in gram_low]
            mixing = [(second * a + third * s).astype(BF) for a, s in zip(gram, square)]
            current = [
                first * x + dot(b, y, 1, 0) for x, b, y in zip(current, mixing, low)
            ]
        for i in range(3):
            weights[i] = weights[i] - step_ref[0] * current[i]

    def sq_copy(group, target, slot):
        return remote(
            squares.at[group, head],
            squares.at[group, slot],
            send_sq.at[group, target],
            recv_sq.at[group, slot],
            me,
            target,
        )

    def apply_group(group):
        for a in range(group * members, (group + 1) * members):

            @pl.when(me != a)
            def _():
                q_copy(0, a).wait_recv()

        wb = [weights[i].astype(BF) for i in range(3)]
        normed = rms_rows(
            q_all[group * members : (group + 1) * members].reshape(group_rows, dh)
        )
        gate = dot(normed, wb[0], 1, 0)
        upward = dot(normed, wb[1], 1, 0)
        hidden = (gate * jax.nn.sigmoid(gate) * upward).astype(BF)
        result = dot(hidden, wb[2], 1, 0)
        fast[group] = result
        line = dot(jnp.ones((8, dh), BF), (result * result).astype(BF), 1, 1)
        squares[group, head] = jnp.zeros(squares.shape[2:], F32)
        for i in range(group_rows // LANES):
            squares[group, head, i : i + 1, :] = line[0:1, i * LANES : (i + 1) * LANES]
        for h in range(head_count):

            @pl.when(head != h)
            def _():
                sq_copy(group, h, head).start()

    def finish_group(group):
        for a in range(group * members, (group + 1) * members):

            @pl.when(me != a)
            def _():
                att_copy(0, a).wait_recv()

        for h in range(head_count):

            @pl.when(head != h)
            def _():
                sq_copy(group, h, h).wait_recv()

        total = squares[group, 0]
        for h in range(1, head_count):
            total = total + squares[group, h]
        factor = jnp.transpose(lax.rsqrt(total / width + 1e-06))
        gain = gain_ref[...]
        piece = min(LANES, out_rows)
        for start in range(0, group_rows, piece):
            a, begin = group * members + start // out_rows, start % out_rows
            lane, low = start // LANES, start % LANES
            out_ref[a, begin : begin + piece, :] = (
                att_all[a, begin : begin + piece, :].astype(F32)
                + gain
                * fast[group, start : start + piece, :]
                * factor[low : low + piece, lane : lane + 1]
            )

    for group in range(GROUPS):

        @pl.when(own_group == group)
        def _():
            group_sums(group)
            if group == 0:
                send_inputs()
            else:
                attend_half(True)

        if group == 0:

            @pl.when(own_group != 0)
            def _():
                send_inputs()
                attend_half(False)

        else:
            if group == 1:

                @pl.when(own_group == 0)
                def _():
                    attend_half(False)
                    attend_half(True)

            apply_group(group - 1)
        collect_sums(group)
        update(group)
    apply_group(GROUPS - 1)
    for group in range(GROUPS):
        finish_group(group)

    @pl.when(me < seq_count - 1)
    def _():
        tail_copy(0, me + 1).wait_send()
        tail_copy(1, me + 1).wait_send()

    for d in range(seq_count):

        @pl.when(me != d)
        def _():
            q_copy(d, me).wait_send()
            att_copy(d, me).wait_send()

    for m in range(members):

        @pl.when(own_member != m)
        def _():
            part_copy(own_group, m, own_member).wait_send()
            for group in range(GROUPS):
                sum_copy(
                    group, own_member, send_sum.at[group, m], own_group * members + m
                ).wait_send()

    for other in range(GROUPS):

        @pl.when(own_group != other)
        def _():
            sum_copy(
                own_group, own_member, send_cross.at[other], other * members + own_member
            ).wait_send()

    for group in range(GROUPS):
        for h in range(head_count):

            @pl.when(head != h)
            def _():
                sq_copy(group, h, head).wait_send()


def solution(mesh):
    seq_count, head_count = mesh.shape["seq"], mesh.shape["head"]

    def on_device(
        queries, key_vectors, value_vectors, fast_gate, fast_up, fast_down, step_sizes, out_gain
    ):
        rows, dh = queries.shape
        window = rows // 2
        members = seq_count // GROUPS
        out_rows = rows // seq_count
        group_rows = rows // GROUPS
        chunk = -(-3 * dh // (members * 16)) * 16
        lines = max(8, group_rows // LANES)
        dma = pltpu.SemaphoreType.DMA
        vmem = pl.BlockSpec(memory_space=pltpu.VMEM)
        smem = pl.BlockSpec(memory_space=pltpu.SMEM)
        return pl.pallas_call(
            functools.partial(kernel, seq_count, head_count),
            out_shape=jax.ShapeDtypeStruct((seq_count, out_rows, dh), F32),
            in_specs=[vmem] * 6 + [smem, vmem],
            out_specs=vmem,
            scratch_shapes=[
                pltpu.VMEM((seq_count, out_rows, dh), BF),
                pltpu.VMEM((rows, dh), BF),
                pltpu.VMEM((seq_count, out_rows, dh), BF),
                pltpu.VMEM((window, dh), BF),
                pltpu.VMEM((window, dh), BF),
                pltpu.VMEM((dh, rows), BF),
                pltpu.VMEM((dh, rows), BF),
                pltpu.VMEM((members * chunk, dh), F32),
                pltpu.VMEM((members * chunk, dh), BF),
                pltpu.VMEM((members, chunk, dh), BF),
                pltpu.VMEM((GROUPS, members * chunk, dh), BF),
                pltpu.VMEM((3, dh, dh), F32),
                pltpu.VMEM((GROUPS, group_rows, dh), F32),
                pltpu.VMEM((GROUPS, head_count, lines, LANES), F32),
                dma((seq_count,)),
                dma((seq_count,)),
                dma((seq_count,)),
                dma((seq_count,)),
                dma((2,)),
                dma((2,)),
                dma((members,)),
                dma((members,)),
                dma((GROUPS, members)),
                dma((GROUPS, members)),
                dma((GROUPS,)),
                dma((GROUPS, head_count)),
                dma((GROUPS, head_count)),
            ],
            compiler_params=pltpu.CompilerParams(
                collective_id=0, has_side_effects=True, vmem_limit_bytes=48 * 1024 * 1024
            ),
        )(
            queries,
            key_vectors,
            value_vectors,
            fast_gate,
            fast_up,
            fast_down,
            step_sizes,
            out_gain.reshape(1, dh),
        )

    in_specs = (
        P("seq", "head"),
        P("seq", "head"),
        P("seq", "head"),
        P("head", None, None),
        P("head", None, None),
        P("head", None, None),
        P("head"),
        P("head"),
    )
    return jax.shard_map(
        on_device, mesh=mesh, in_specs=in_specs, out_specs=P(None, "seq", "head"), check_vma=False
    )
```

```python
import functools
import math

import jax
import jax.numpy as jnp
from jax import lax
from jax.experimental import pallas as pl
from jax.experimental.pallas import tpu as pltpu
from jax.sharding import PartitionSpec as P

GROUPS = 2
NS_ITERS = 4

newton_coefs = (3.4445, -4.775, 2.0315)
MESH = pl.DeviceIdType.MESH
BF = jnp.bfloat16
F32 = jnp.float32


def dot(left, right, left_dim, right_dim):
    return lax.dot_general(
        left, right, (((left_dim,), (right_dim,)), ((), ())), preferred_element_type=F32
    )


def rms_columns(array):
    array = array.astype(F32)
    return (array * lax.rsqrt(jnp.mean(array * array, 0, keepdims=True) + 1e-06)).astype(BF)


def kernel(
    seq_count,
    head_count,
    q_hbm,
    k_hbm,
    v_hbm,
    gate_hbm,
    up_hbm,
    down_hbm,
    step_ref,
    gain_ref,
    out_ref,
    q_ref,
    k_ref,
    v_ref,
    first_weights,
    key_rows,
    tail_rows,
    q_own,
    q_all,
    att_own,
    att_all,
    tail_k,
    tail_v,
    key_t,
    val_t,
    grad_f,
    grad_b,
    grad_in,
    sums,
    weights,
    fast,
    squares,
    send_q,
    recv_q,
    send_att,
    recv_att,
    send_tail,
    recv_tail,
    send_part,
    recv_part,
    send_sum,
    recv_sum,
    send_cross,
    send_sq,
    recv_sq,
    load,
):
    dh, rows = q_ref.shape
    window = rows // 2
    members = seq_count // GROUPS
    out_rows = rows // seq_count
    chunk = grad_in.shape[1]
    width = dh * head_count
    me = lax.axis_index("seq")
    head = lax.axis_index("head")
    own_group = me // members
    own_member = lax.rem(me, members)

    def remote(src, dst, send, recv, seq, hd):
        return pltpu.make_async_remote_copy(
            src_ref=src,
            dst_ref=dst,
            send_sem=send,
            recv_sem=recv,
            device_id=(seq, hd),
            device_id_type=MESH,
        )

    def rows_of(index, size):
        return pl.ds(pl.multiple_of(index * size, size), size)

    barrier = pltpu.get_barrier_semaphore()
    for d in range(1, seq_count):
        pl.semaphore_signal(
            barrier, inc=1, device_id=(lax.rem(me + d, seq_count), head), device_id_type=MESH
        )
    for d in range(1, head_count):
        pl.semaphore_signal(
            barrier, inc=1, device_id=(me, lax.rem(head + d, head_count)), device_id_type=MESH
        )

    loads = [
        pltpu.make_async_copy(src, dst, load.at[i])
        for i, (src, dst) in enumerate(
            (
                (k_hbm, k_ref),
                (v_hbm, v_ref),
                (gate_hbm.at[0], first_weights.at[0]),
                (up_hbm.at[0], first_weights.at[1]),
                (down_hbm.at[0], first_weights.at[2]),
                (q_hbm, q_ref),
            )
        )
    ]
    for copy in loads:
        copy.start()
    for copy in loads:
        copy.wait()
    key_t[...] = rms_columns(k_ref[...])
    val_t[...] = -v_ref[...]
    weights[0] = jnp.transpose(first_weights[0])
    weights[1] = jnp.transpose(first_weights[1])
    weights[2] = first_weights[2]
    spare = members * chunk - 3 * dh
    if spare:
        grad_f[3 * dh :, :] = jnp.zeros((spare, dh), F32)
        grad_b[3 * dh :, :] = jnp.zeros((spare, dh), BF)

    @pl.when(me == 0)
    def _():
        tail_k[...] = jnp.zeros(tail_k.shape, BF)
        tail_v[...] = jnp.zeros(tail_v.shape, BF)

    pl.semaphore_wait(barrier, seq_count + head_count - 2)

    def q_copy(d, slot):
        return remote(
            q_own.at[d],
            q_all.at[slot],
            send_q.at[d],
            recv_q.at[slot],
            d,
            head,
        )

    def tail_copy(which, target):
        source = (k_ref, v_ref)[which]
        landing = (tail_k, tail_v)[which]
        return remote(
            source.at[:, pl.ds(rows - window, window)],
            landing,
            send_tail.at[which],
            recv_tail.at[which],
            target,
            head,
        )

    def send_inputs():
        @pl.when(me < seq_count - 1)
        def _():
            tail_copy(0, me + 1).start()
            tail_copy(1, me + 1).start()

        for d in range(seq_count):
            q_own[d] = q_ref[:, d * out_rows : (d + 1) * out_rows]

            @pl.when(me != d)
            def _():
                q_copy(d, me).start()

        q_all[me] = q_own[me]

    scale = 1.0 / math.sqrt(dh)
    block = min(256, window)

    def attend(start):
        if start < window:
            keys = jnp.concatenate([tail_rows[start:, :], key_rows[: start + block, :]], 0)
            values = jnp.concatenate([tail_v[:, start:], v_ref[:, : start + block]], 1)
        else:
            keys = key_rows[start - window : start + block, :]
            values = v_ref[:, start - window : start + block]
        scores = dot(keys, q_ref[:, start : start + block], 1, 0) * scale
        key = lax.broadcasted_iota(jnp.int32, scores.shape, 0)
        query = lax.broadcasted_iota(jnp.int32, scores.shape, 1)
        allowed = (key <= query + window) & (key > query)
        if start < window:
            allowed = allowed & (key >= jnp.where(me == 0, window - start, 0))
        scores = jnp.where(allowed, scores, -1e30)
        highest = jnp.max(scores, 0, keepdims=True)
        expo = jnp.where(allowed, jnp.exp(scores - highest), 0.0)
        probs = (expo / jnp.sum(expo, 0, keepdims=True)).astype(BF)
        mixed = dot(values, probs, 1, 0).astype(BF)
        piece = min(block, out_rows)
        for begin in range(0, block, piece):
            d, low = (start + begin) // out_rows, (start + begin) % out_rows
            att_own[d, :, low : low + piece] = mixed[:, begin : begin + piece]

    def att_copy(d, slot):
        return remote(
            att_own.at[d],
            att_all.at[slot],
            send_att.at[d],
            recv_att.at[slot],
            d,
            head,
        )

    def attend_half(first):
        begin = 0 if first else window
        if first:

            @pl.when(me > 0)
            def _():
                tail_copy(0, me).wait_recv()
                tail_copy(1, me).wait_recv()

            tail_rows[...] = jnp.transpose(tail_k[...])
        else:
            key_rows[...] = jnp.transpose(k_ref[...])

        for start in range(begin, begin + window, block):
            attend(start)
        for d in range(begin // out_rows, (begin + window) // out_rows):

            @pl.when(me != d)
            def _():
                att_copy(d, me).start()

            @pl.when(me == d)
            def _():
                att_all[d] = att_own[d]

    token_block = min(512, rows)

    def gradients():
        wb = [weights[i].astype(BF) for i in range(3)]
        totals = [None] * 3
        for start in range(0, rows, token_block):
            keys = key_t[:, start : start + token_block]
            values = val_t[:, start : start + token_block]
            gate = dot(wb[0], keys, 1, 0)
            upward = dot(wb[1], keys, 1, 0)
            back = dot(wb[2], values, 1, 0)
            sigma = jax.nn.sigmoid(gate)
            active = gate * sigma
            hidden = (active * upward).astype(BF)
            slope = sigma * (1.0 + gate * (1.0 - sigma))
            grad_gate = (back * upward * slope).astype(BF)
            grad_up = (back * active).astype(BF)
            parts = [
                dot(grad_gate, keys, 1, 1),
                dot(grad_up, keys, 1, 1),
                dot(hidden, values, 1, 1),
            ]
            totals = [p if t is None else t + p for t, p in zip(totals, parts)]
        for i in range(3):
            grad_f[i * dh : (i + 1) * dh, :] = totals[i]
            grad_b[i * dh : (i + 1) * dh, :] = totals[i].astype(BF)

    def part_copy(group, target, slot):
        return remote(
            grad_b.at[pl.ds(target * chunk, chunk), :],
            grad_in.at[slot],
            send_part.at[target],
            recv_part.at[slot],
            group * members + target,
            head,
        )

    def sum_copy(group, piece, send, seq):
        place = sums.at[group, rows_of(piece, chunk), :]
        return remote(place, place, send, recv_sum.at[group, piece], seq, head)

    def spread(group):
        for m in range(members):

            @pl.when(own_member != m)
            def _():
                sum_copy(
                    group, own_member, send_sum.at[group, m], own_group * members + m
                ).start()

    def group_sums(group):
        gradients()
        for m in range(members):

            @pl.when(own_member != m)
            def _():
                part_copy(group, m, own_member).start()

        place = rows_of(own_member, chunk)
        grad_in[own_member] = jnp.zeros(grad_in.shape[1:], BF)
        for m in range(members):

            @pl.when(own_member != m)
            def _():
                part_copy(group, m, m).wait_recv()

        total = grad_f[place, :]
        for m in range(members):
            total = total + grad_in[m].astype(F32)
        sums[group, place, :] = total.astype(BF)
        for other in range(GROUPS):
            if other != group:
                sum_copy(
                    group, own_member, send_cross.at[other], other * members + own_member
                ).start()
        spread(group)

    def collect_sums(group):
        @pl.when(own_group != group)
        def _():
            sum_copy(group, own_member, send_cross.at[group], me).wait_recv()
            spread(group)

        for m in range(members):

            @pl.when(own_member != m)
            def _():
                sum_copy(group, m, send_cross.at[group], me).wait_recv()

    def update(group):
        first, second, third = newton_coefs
        current = []
        for i in range(3):
            grads = sums[group, i * dh : (i + 1) * dh, :].astype(F32)
            total = jnp.sum(jnp.sum(grads * grads, 1, keepdims=True), 0, keepdims=True)
            current.append(grads * lax.rsqrt(total + 1e-06))
        for repeat in range(NS_ITERS):
            low = [x.astype(BF) for x in current]
            gram = [dot(x, x, 1, 1) for x in low]
            gram_low = [a.astype(BF) for a in gram]
            square = [dot(a, a, 1, 0) for a in gram_low]
            mixing = [(second * a + third * s).astype(BF) for a, s in zip(gram, square)]
            current = [
                first * x + dot(b, y, 1, 0) for x, b, y in zip(current, mixing, low)
            ]
        for i in range(3):
            weights[i] = weights[i] - step_ref[0] * current[i]

    def sq_copy(group, target, slot):
        return remote(
            squares.at[group, head],
            squares.at[group, slot],
            send_sq.at[group, target],
            recv_sq.at[group, slot],
            me,
            target,
        )

    def apply_group(group):
        for a in range(group * members, (group + 1) * members):

            @pl.when(me != a)
            def _():
                q_copy(0, a).wait_recv()

        wb = [weights[i].astype(BF) for i in range(3)]
        down = jnp.transpose(weights[2]).astype(BF)
        for place, a in enumerate(range(group * members, (group + 1) * members)):
            normed = rms_columns(q_all[a])
            gate = dot(wb[0], normed, 1, 0)
            upward = dot(wb[1], normed, 1, 0)
            hidden = (gate * jax.nn.sigmoid(gate) * upward).astype(BF)
            result = dot(down, hidden, 1, 0)
            fast[a] = result
            squares[group, head, place : place + 1, :] = jnp.sum(
                result * result, 0, keepdims=True
            )
        for h in range(head_count):

            @pl.when(head != h)
            def _():
                sq_copy(group, h, head).start()

    def finish_group(group):
        for a in range(group * members, (group + 1) * members):

            @pl.when(me != a)
            def _():
                att_copy(0, a).wait_recv()

        for h in range(head_count):

            @pl.when(head != h)
            def _():
                sq_copy(group, h, h).wait_recv()

        total = squares[group, 0]
        for h in range(1, head_count):
            total = total + squares[group, h]
        factor = lax.rsqrt(total / width + 1e-06)
        gain = jnp.transpose(jnp.broadcast_to(gain_ref[...].reshape(1, dh), (8, dh)))[:, 0:1]
        for place, a in enumerate(range(group * members, (group + 1) * members)):
            out_ref[a] = att_all[a].astype(F32) + gain * fast[a] * factor[place : place + 1, :]

    for group in range(GROUPS):

        @pl.when(own_group == group)
        def _():
            group_sums(group)
            if group == 0:
                send_inputs()
            else:
                attend_half(True)

        if group == 0:

            @pl.when(own_group != 0)
            def _():
                send_inputs()
                attend_half(False)

        else:
            if group == 1:

                @pl.when(own_group == 0)
                def _():
                    attend_half(False)
                    attend_half(True)

            apply_group(group - 1)
        collect_sums(group)
        update(group)
    apply_group(GROUPS - 1)
    for group in range(GROUPS):
        finish_group(group)

    @pl.when(me < seq_count - 1)
    def _():
        tail_copy(0, me + 1).wait_send()
        tail_copy(1, me + 1).wait_send()

    for d in range(seq_count):

        @pl.when(me != d)
        def _():
            q_copy(d, me).wait_send()
            att_copy(d, me).wait_send()

    for m in range(members):

        @pl.when(own_member != m)
        def _():
            part_copy(own_group, m, own_member).wait_send()
            for group in range(GROUPS):
                sum_copy(
                    group, own_member, send_sum.at[group, m], own_group * members + m
                ).wait_send()

    for other in range(GROUPS):

        @pl.when(own_group != other)
        def _():
            sum_copy(
                own_group, own_member, send_cross.at[other], other * members + own_member
            ).wait_send()

    for group in range(GROUPS):
        for h in range(head_count):

            @pl.when(head != h)
            def _():
                sq_copy(group, h, head).wait_send()


def solution(mesh):
    seq_count, head_count = mesh.shape["seq"], mesh.shape["head"]

    def on_device(
        queries, key_vectors, value_vectors, fast_gate, fast_up, fast_down, step_sizes, out_gain
    ):
        rows, dh = queries.shape
        window = rows // 2
        members = seq_count // GROUPS
        out_rows = rows // seq_count
        chunk = -(-3 * dh // (members * 16)) * 16
        dma = pltpu.SemaphoreType.DMA
        vmem = pl.BlockSpec(memory_space=pltpu.VMEM)
        smem = pl.BlockSpec(memory_space=pltpu.SMEM)
        return pl.pallas_call(
            functools.partial(kernel, seq_count, head_count),
            out_shape=jax.ShapeDtypeStruct((seq_count, dh, out_rows), F32),
            in_specs=[pl.BlockSpec(memory_space=pltpu.HBM)] * 6 + [smem, vmem],
            out_specs=vmem,
            scratch_shapes=[
                pltpu.VMEM((dh, rows), BF),
                pltpu.VMEM((dh, rows), BF),
                pltpu.VMEM((dh, rows), BF),
                pltpu.VMEM((3, dh, dh), F32),
                pltpu.VMEM((rows, dh), BF),
                pltpu.VMEM((window, dh), BF),
                pltpu.VMEM((seq_count, dh, out_rows), BF),
                pltpu.VMEM((seq_count, dh, out_rows), BF),
                pltpu.VMEM((seq_count, dh, out_rows), BF),
                pltpu.VMEM((seq_count, dh, out_rows), BF),
                pltpu.VMEM((dh, window), BF),
                pltpu.VMEM((dh, window), BF),
                pltpu.VMEM((dh, rows), BF),
                pltpu.VMEM((dh, rows), BF),
                pltpu.VMEM((members * chunk, dh), F32),
                pltpu.VMEM((members * chunk, dh), BF),
                pltpu.VMEM((members, chunk, dh), BF),
                pltpu.VMEM((GROUPS, members * chunk, dh), BF),
                pltpu.VMEM((3, dh, dh), F32),
                pltpu.VMEM((seq_count, dh, out_rows), F32),
                pltpu.VMEM((GROUPS, head_count, members, out_rows), F32),
                dma((seq_count,)),
                dma((seq_count,)),
                dma((seq_count,)),
                dma((seq_count,)),
                dma((2,)),
                dma((2,)),
                dma((members,)),
                dma((members,)),
                dma((GROUPS, members)),
                dma((GROUPS, members)),
                dma((GROUPS,)),
                dma((GROUPS, head_count)),
                dma((GROUPS, head_count)),
                dma((6,)),
            ],
            compiler_params=pltpu.CompilerParams(
                collective_id=0, has_side_effects=True, vmem_limit_bytes=60 * 1024 * 1024
            ),
        )(
            queries.T,
            key_vectors.T,
            value_vectors.T,
            fast_gate,
            fast_up,
            fast_down,
            step_sizes,
            out_gain,
        ).swapaxes(1, 2)

    in_specs = (
        P("seq", "head"),
        P("seq", "head"),
        P("seq", "head"),
        P("head", None, None),
        P("head", None, None),
        P("head", None, None),
        P("head"),
        P("head"),
    )
    return jax.shard_map(
        on_device, mesh=mesh, in_specs=in_specs, out_specs=P(None, "seq", "head"), check_vma=False
    )
```

```python
import functools
import math

import jax
import jax.numpy as jnp
from jax import lax
from jax.experimental import pallas as pl
from jax.experimental.pallas import tpu as pltpu
from jax.sharding import PartitionSpec as P

GROUPS = 2
NS_ITERS = 4

newton_coefs = (3.4445, -4.775, 2.0315)
MESH = pl.DeviceIdType.MESH
BF = jnp.bfloat16
F32 = jnp.float32


def dot(left, right, left_dim, right_dim):
    return lax.dot_general(
        left, right, (((left_dim,), (right_dim,)), ((), ())), preferred_element_type=F32
    )


def rms_columns(array):
    array = array.astype(F32)
    return (array * lax.rsqrt(jnp.mean(array * array, 0, keepdims=True) + 1e-06)).astype(BF)


def kernel(
    seq_count,
    head_count,
    q_hbm,
    k_hbm,
    v_hbm,
    gate_hbm,
    up_hbm,
    down_hbm,
    step_ref,
    gain_ref,
    out_ref,
    q_ref,
    k_ref,
    v_ref,
    first_weights,
    key_rows,
    tail_rows,
    q_own,
    q_all,
    att_own,
    att_all,
    tail_k,
    tail_v,
    key_t,
    val_t,
    grad_f,
    grad_b,
    grad_in,
    sums,
    weights,
    fast,
    squares,
    send_q,
    recv_q,
    send_att,
    recv_att,
    send_tail,
    recv_tail,
    send_part,
    recv_part,
    send_sum,
    recv_sum,
    send_cross,
    send_sq,
    recv_sq,
    load,
):
    dh, rows = q_ref.shape
    window = rows // 2
    members = seq_count // GROUPS
    out_rows = rows // seq_count
    chunk = grad_in.shape[2]
    matrix_rows = members * chunk
    width = dh * head_count
    me = lax.axis_index("seq")
    head = lax.axis_index("head")
    own_group = me // members
    own_member = lax.rem(me, members)

    def remote(src, dst, send, recv, seq, hd):
        return pltpu.make_async_remote_copy(
            src_ref=src,
            dst_ref=dst,
            send_sem=send,
            recv_sem=recv,
            device_id=(seq, hd),
            device_id_type=MESH,
        )

    def rows_of(index, size):
        return pl.ds(pl.multiple_of(index * size, size), size)

    barrier = pltpu.get_barrier_semaphore()
    for d in range(1, seq_count):
        pl.semaphore_signal(
            barrier, inc=1, device_id=(lax.rem(me + d, seq_count), head), device_id_type=MESH
        )
    for d in range(1, head_count):
        pl.semaphore_signal(
            barrier, inc=1, device_id=(me, lax.rem(head + d, head_count)), device_id_type=MESH
        )

    loads = [
        pltpu.make_async_copy(src, dst, load.at[i])
        for i, (src, dst) in enumerate(
            (
                (k_hbm, k_ref),
                (v_hbm, v_ref),
                (gate_hbm.at[0], first_weights.at[0]),
                (up_hbm.at[0], first_weights.at[1]),
                (down_hbm.at[0], first_weights.at[2]),
                (q_hbm, q_ref),
            )
        )
    ]
    for copy in loads:
        copy.start()
    for copy in loads:
        copy.wait()
    key_t[...] = rms_columns(k_ref[...])
    val_t[...] = -v_ref[...]
    weights[0] = jnp.transpose(first_weights[0])
    weights[1] = jnp.transpose(first_weights[1])
    weights[2] = first_weights[2]
    spare = matrix_rows - dh
    if spare:
        for i in range(3):
            grad_f[i, dh:, :] = jnp.zeros((spare, dh), F32)
            grad_b[i, dh:, :] = jnp.zeros((spare, dh), BF)

    @pl.when(me == 0)
    def _():
        tail_k[...] = jnp.zeros(tail_k.shape, BF)
        tail_v[...] = jnp.zeros(tail_v.shape, BF)

    pl.semaphore_wait(barrier, seq_count + head_count - 2)

    def q_copy(d, slot):
        return remote(
            q_own.at[d],
            q_all.at[slot],
            send_q.at[d],
            recv_q.at[slot],
            d,
            head,
        )

    def tail_copy(which, target):
        source = (k_ref, v_ref)[which]
        landing = (tail_k, tail_v)[which]
        return remote(
            source.at[:, pl.ds(rows - window, window)],
            landing,
            send_tail.at[which],
            recv_tail.at[which],
            target,
            head,
        )

    def send_inputs():
        @pl.when(me < seq_count - 1)
        def _():
            tail_copy(0, me + 1).start()
            tail_copy(1, me + 1).start()

        for d in range(seq_count):
            q_own[d] = q_ref[:, d * out_rows : (d + 1) * out_rows]

            @pl.when(me != d)
            def _():
                q_copy(d, me).start()

        q_all[me] = q_own[me]

    scale = 1.0 / math.sqrt(dh)
    block = min(256, window)

    def attend(start):
        if start < window:
            keys = jnp.concatenate([tail_rows[start:, :], key_rows[: start + block, :]], 0)
            values = jnp.concatenate([tail_v[:, start:], v_ref[:, : start + block]], 1)
        else:
            keys = key_rows[start - window : start + block, :]
            values = v_ref[:, start - window : start + block]
        scores = dot(keys, q_ref[:, start : start + block], 1, 0) * scale
        key = lax.broadcasted_iota(jnp.int32, scores.shape, 0)
        query = lax.broadcasted_iota(jnp.int32, scores.shape, 1)
        allowed = (key <= query + window) & (key > query)
        if start < window:
            allowed = allowed & (key >= jnp.where(me == 0, window - start, 0))
        scores = jnp.where(allowed, scores, -1e30)
        highest = jnp.max(scores, 0, keepdims=True)
        expo = jnp.where(allowed, jnp.exp(scores - highest), 0.0)
        probs = (expo / jnp.sum(expo, 0, keepdims=True)).astype(BF)
        mixed = dot(values, probs, 1, 0).astype(BF)
        piece = min(block, out_rows)
        for begin in range(0, block, piece):
            d, low = (start + begin) // out_rows, (start + begin) % out_rows
            att_own[d, :, low : low + piece] = mixed[:, begin : begin + piece]

    def att_copy(d, slot):
        return remote(
            att_own.at[d],
            att_all.at[slot],
            send_att.at[d],
            recv_att.at[slot],
            d,
            head,
        )

    def attend_half(first):
        begin = 0 if first else window
        if first:

            @pl.when(me > 0)
            def _():
                tail_copy(0, me).wait_recv()
                tail_copy(1, me).wait_recv()

            tail_rows[...] = jnp.transpose(tail_k[...])
        else:
            key_rows[...] = jnp.transpose(k_ref[...])

        for start in range(begin, begin + window, block):
            attend(start)
        for d in range(begin // out_rows, (begin + window) // out_rows):

            @pl.when(me != d)
            def _():
                att_copy(d, me).start()

            @pl.when(me == d)
            def _():
                att_all[d] = att_own[d]

    token_block = min(512, rows)

    def gradients():
        wb = [weights[i].astype(BF) for i in range(3)]
        totals = [None] * 3
        for start in range(0, rows, token_block):
            keys = key_t[:, start : start + token_block]
            values = val_t[:, start : start + token_block]
            gate = dot(wb[0], keys, 1, 0)
            upward = dot(wb[1], keys, 1, 0)
            back = dot(wb[2], values, 1, 0)
            sigma = jax.nn.sigmoid(gate)
            active = gate * sigma
            hidden = (active * upward).astype(BF)
            slope = sigma * (1.0 + gate * (1.0 - sigma))
            grad_gate = (back * upward * slope).astype(BF)
            grad_up = (back * active).astype(BF)
            parts = [
                dot(grad_gate, keys, 1, 1),
                dot(grad_up, keys, 1, 1),
                dot(hidden, values, 1, 1),
            ]
            totals = [p if t is None else t + p for t, p in zip(totals, parts)]
        for i in range(3):
            grad_f[i, :dh, :] = totals[i]
            grad_b[i, :dh, :] = totals[i].astype(BF)

    def part_copy(group, i, target, slot):
        return remote(
            grad_b.at[i, pl.ds(target * chunk, chunk), :],
            grad_in.at[i, slot],
            send_part.at[i, target],
            recv_part.at[i, slot],
            group * members + target,
            head,
        )

    def sum_copy(group, i, piece, send, seq):
        place = sums.at[group, i, rows_of(piece, chunk), :]
        return remote(place, place, send, recv_sum.at[group, i, piece], seq, head)

    def spread(group, i):
        for m in range(members):

            @pl.when(own_member != m)
            def _():
                sum_copy(
                    group, i, own_member, send_sum.at[group, i, m], own_group * members + m
                ).start()

    def group_sums(group):
        gradients()
        for i in range(3):
            for m in range(members):

                @pl.when(own_member != m)
                def _():
                    part_copy(group, i, m, own_member).start()

            grad_in[i, own_member] = jnp.zeros(grad_in.shape[2:], BF)

        place = rows_of(own_member, chunk)
        for i in range(3):
            for m in range(members):

                @pl.when(own_member != m)
                def _():
                    part_copy(group, i, m, m).wait_recv()

            total = grad_f[i, place, :]
            for m in range(members):
                total = total + grad_in[i, m].astype(F32)
            sums[group, i, place, :] = total.astype(BF)
            for other in range(GROUPS):
                if other != group:
                    sum_copy(
                        group,
                        i,
                        own_member,
                        send_cross.at[other, i],
                        other * members + own_member,
                    ).start()
            spread(group, i)

    def collect_sums(group, matrices):
        for i in matrices:

            @pl.when(own_group != group)
            def _():
                sum_copy(group, i, own_member, send_cross.at[group, i], me).wait_recv()
                spread(group, i)

        for i in matrices:
            for m in range(members):

                @pl.when(own_member != m)
                def _():
                    sum_copy(group, i, m, send_cross.at[group, i], me).wait_recv()

    def update(group, matrices):
        first, second, third = newton_coefs
        current = []
        for i in matrices:
            grads = sums[group, i, :dh, :].astype(F32)
            total = jnp.sum(jnp.sum(grads * grads, 1, keepdims=True), 0, keepdims=True)
            current.append(grads * lax.rsqrt(total + 1e-06))
        for repeat in range(NS_ITERS):
            low = [x.astype(BF) for x in current]
            gram = [dot(x, x, 1, 1) for x in low]
            gram_low = [a.astype(BF) for a in gram]
            square = [dot(a, a, 1, 0) for a in gram_low]
            mixing = [(second * a + third * s).astype(BF) for a, s in zip(gram, square)]
            current = [
                first * x + dot(b, y, 1, 0) for x, b, y in zip(current, mixing, low)
            ]
        for i, x in zip(matrices, current):
            weights[i] = weights[i] - step_ref[0] * x

    def sq_copy(group, target, slot):
        return remote(
            squares.at[group, head],
            squares.at[group, slot],
            send_sq.at[group, target],
            recv_sq.at[group, slot],
            me,
            target,
        )

    def apply_group(group):
        for a in range(group * members, (group + 1) * members):

            @pl.when(me != a)
            def _():
                q_copy(0, a).wait_recv()

        wb = [weights[i].astype(BF) for i in range(3)]
        down = jnp.transpose(weights[2]).astype(BF)
        for place, a in enumerate(range(group * members, (group + 1) * members)):
            normed = rms_columns(q_all[a])
            gate = dot(wb[0], normed, 1, 0)
            upward = dot(wb[1], normed, 1, 0)
            hidden = (gate * jax.nn.sigmoid(gate) * upward).astype(BF)
            result = dot(down, hidden, 1, 0)
            fast[a] = result
            squares[group, head, place : place + 1, :] = jnp.sum(
                result * result, 0, keepdims=True
            )
        for h in range(head_count):

            @pl.when(head != h)
            def _():
                sq_copy(group, h, head).start()

    def finish_group(group):
        for a in range(group * members, (group + 1) * members):

            @pl.when(me != a)
            def _():
                att_copy(0, a).wait_recv()

        for h in range(head_count):

            @pl.when(head != h)
            def _():
                sq_copy(group, h, h).wait_recv()

        total = squares[group, 0]
        for h in range(1, head_count):
            total = total + squares[group, h]
        factor = lax.rsqrt(total / width + 1e-06)
        gain = jnp.transpose(jnp.broadcast_to(gain_ref[...].reshape(1, dh), (8, dh)))[:, 0:1]
        for place, a in enumerate(range(group * members, (group + 1) * members)):
            out_ref[a] = att_all[a].astype(F32) + gain * fast[a] * factor[place : place + 1, :]

    for group in range(GROUPS):

        @pl.when(own_group == group)
        def _():
            group_sums(group)
            if group == 0:
                send_inputs()
            else:
                attend_half(True)

        if group == 0:

            @pl.when(own_group != 0)
            def _():
                send_inputs()
                attend_half(False)

        else:
            if group == 1:

                @pl.when(own_group == 0)
                def _():
                    attend_half(False)
                    attend_half(True)

            apply_group(group - 1)
        for matrices in ((0,), (1, 2)):
            collect_sums(group, matrices)
            update(group, matrices)
    apply_group(GROUPS - 1)
    for group in range(GROUPS):
        finish_group(group)

    @pl.when(me < seq_count - 1)
    def _():
        tail_copy(0, me + 1).wait_send()
        tail_copy(1, me + 1).wait_send()

    for d in range(seq_count):

        @pl.when(me != d)
        def _():
            q_copy(d, me).wait_send()
            att_copy(d, me).wait_send()

    for i in range(3):
        for m in range(members):

            @pl.when(own_member != m)
            def _():
                part_copy(own_group, i, m, own_member).wait_send()
                for group in range(GROUPS):
                    sum_copy(
                        group, i, own_member, send_sum.at[group, i, m], own_group * members + m
                    ).wait_send()

        for other in range(GROUPS):

            @pl.when(own_group != other)
            def _():
                sum_copy(
                    own_group,
                    i,
                    own_member,
                    send_cross.at[other, i],
                    other * members + own_member,
                ).wait_send()

    for group in range(GROUPS):
        for h in range(head_count):

            @pl.when(head != h)
            def _():
                sq_copy(group, h, head).wait_send()


def solution(mesh):
    seq_count, head_count = mesh.shape["seq"], mesh.shape["head"]

    def on_device(
        queries, key_vectors, value_vectors, fast_gate, fast_up, fast_down, step_sizes, out_gain
    ):
        rows, dh = queries.shape
        window = rows // 2
        members = seq_count // GROUPS
        out_rows = rows // seq_count
        chunk = -(-dh // (members * 16)) * 16
        dma = pltpu.SemaphoreType.DMA
        vmem = pl.BlockSpec(memory_space=pltpu.VMEM)
        smem = pl.BlockSpec(memory_space=pltpu.SMEM)
        return pl.pallas_call(
            functools.partial(kernel, seq_count, head_count),
            out_shape=jax.ShapeDtypeStruct((seq_count, dh, out_rows), F32),
            in_specs=[pl.BlockSpec(memory_space=pltpu.HBM)] * 6 + [smem, vmem],
            out_specs=vmem,
            scratch_shapes=[
                pltpu.VMEM((dh, rows), BF),
                pltpu.VMEM((dh, rows), BF),
                pltpu.VMEM((dh, rows), BF),
                pltpu.VMEM((3, dh, dh), F32),
                pltpu.VMEM((rows, dh), BF),
                pltpu.VMEM((window, dh), BF),
                pltpu.VMEM((seq_count, dh, out_rows), BF),
                pltpu.VMEM((seq_count, dh, out_rows), BF),
                pltpu.VMEM((seq_count, dh, out_rows), BF),
                pltpu.VMEM((seq_count, dh, out_rows), BF),
                pltpu.VMEM((dh, window), BF),
                pltpu.VMEM((dh, window), BF),
                pltpu.VMEM((dh, rows), BF),
                pltpu.VMEM((dh, rows), BF),
                pltpu.VMEM((3, members * chunk, dh), F32),
                pltpu.VMEM((3, members * chunk, dh), BF),
                pltpu.VMEM((3, members, chunk, dh), BF),
                pltpu.VMEM((GROUPS, 3, members * chunk, dh), BF),
                pltpu.VMEM((3, dh, dh), F32),
                pltpu.VMEM((seq_count, dh, out_rows), F32),
                pltpu.VMEM((GROUPS, head_count, members, out_rows), F32),
                dma((seq_count,)),
                dma((seq_count,)),
                dma((seq_count,)),
                dma((seq_count,)),
                dma((2,)),
                dma((2,)),
                dma((3, members)),
                dma((3, members)),
                dma((GROUPS, 3, members)),
                dma((GROUPS, 3, members)),
                dma((GROUPS, 3)),
                dma((GROUPS, head_count)),
                dma((GROUPS, head_count)),
                dma((6,)),
            ],
            compiler_params=pltpu.CompilerParams(
                collective_id=0, has_side_effects=True, vmem_limit_bytes=60 * 1024 * 1024
            ),
        )(
            queries.T,
            key_vectors.T,
            value_vectors.T,
            fast_gate,
            fast_up,
            fast_down,
            step_sizes,
            out_gain,
        ).swapaxes(1, 2)

    in_specs = (
        P("seq", "head"),
        P("seq", "head"),
        P("seq", "head"),
        P("head", None, None),
        P("head", None, None),
        P("head", None, None),
        P("head"),
        P("head"),
    )
    return jax.shard_map(
        on_device, mesh=mesh, in_specs=in_specs, out_specs=P(None, "seq", "head"), check_vma=False
    )
```
